256 devices in a mesh: row: 16 (over z_hi, x), col: 16 (over z_lo, y, core).
Axes of the slice: x: 4, y: 4, z: 8 (z_hi: 4, z_lo: 2; z = z_hi * 2 + z_lo), core: 2. Of those that a mesh axis runs over, the one named last changes fastest.
Arguments:
- blocks: bfloat16 [48, 896, 896], P('row', 'col'), may hold values from -0.4375 to 0.4375
- eps_occ: float32 [192], P('row'), may hold values from -2 to -0.4
- eps_vir: float32 [224], replicated, may hold values from 0.2 to 2.5
- pairs: int32 [512, 2], P('row'), may hold values from -1 to 47, as said below
Outputs:
- gradient: float32 [48, 896, 896], P('row', 'col')
The draws below stay inside these ranges and needn't reach their ends.
Inputs may be any that keep to these rules, and one draw needn't show every extreme that they name: `pairs`: slot s belongs to row group g = s // 32. A live slot holds two block ids (first, second): first is one of the 3 blocks g * 3 to g * 3 + 2; second is a block of group g not smaller than first, or a block of group g + 1 (mod 16). No pair appears twice. A dead slot holds -1 in both entries. Each row group has exactly 12 live slots.
All inputs are finite; a program needn't handle non-finite values.
Results may differ from the reference program's by a relative error of at most 0.002.
Values may be sent and summed in bfloat16 or wider, within the bound.
A program may use at most 128 MiB of HBM per device.

```python
import jax
import jax.numpy as jnp
from jax import lax

O = 4
V = 224
P_SIZE = 896
BR = 3
PPD = 2
NB = 48
NOCC = 192
PAIRS = 512
N_ROW = 16
N_COL = 16


def draw_pairs(key, part):
    key = jax.random.fold_in(key, 7)
    first_list = []
    second_list = []
    for first_pos in range(BR):
        for second_pos in range(first_pos, BR):
            first_list.append(first_pos)
            second_list.append(second_pos)
        for second_pos in range(BR):
            first_list.append(first_pos)
            second_list.append(BR + second_pos)
    first_table = jnp.array(first_list, jnp.int32)
    second_table = jnp.array(second_list, jnp.int32)
    count_all = len(first_list)
    slots_row = N_COL * PPD
    live_count = min(4 * BR, slots_row)

    def one_row(row_key, group):
        pick_key, device_key = jax.random.split(row_key)
        picked = jax.random.permutation(pick_key, count_all)[:live_count]
        devices = jax.random.permutation(device_key, N_COL)
        number = jnp.arange(live_count, dtype=jnp.int32)
        where_to = devices[number // PPD] * PPD + number % PPD
        first_ids = group * BR + first_table[picked]
        second_ids = (group * BR + second_table[picked]) % (BR * N_ROW)
        filled = jnp.full((slots_row, 2), -1, jnp.int32)
        filled = filled.at[where_to, 0].set(first_ids)
        filled = filled.at[where_to, 1].set(second_ids)
        return filled
    row_keys = jax.random.split(key, N_ROW)
    table = jax.vmap(one_row)(row_keys, jnp.arange(N_ROW, dtype=jnp.int32))
    return table.reshape(N_ROW * slots_row, 2)


def block_levels(stream_key, shape, shards, low, top_value):
    def one(dim, shards_of):
        heights = jax.random.uniform(jax.random.fold_in(jax.random.fold_in(stream_key, 6), dim), (shards_of,), jnp.float32, low / len(shards), top_value / len(shards))
        return jnp.repeat(jnp.exp(heights), shape[dim] // shards_of).reshape((-1,) + (1,) * (len(shape) - dim - 1))

    factor_of = one(*shards[0])
    for cut in shards[1:]:
        factor_of = factor_of * one(*cut)
    return factor_of


def normal_values(key, shape, scale, limit, shards=(), kind=jnp.bfloat16):
    result = scale * jax.random.normal(key, shape, jnp.float32)
    if shards:
        result = result * block_levels(key, shape, shards, -0.22, 0.18)
    return jnp.clip(result, -limit, limit).astype(kind)


def setup_inputs(seed: int = 0) -> dict:
    seeds = jax.random.split(jax.random.key(seed), 5)
    blocks = normal_values(seeds[0], (NB, P_SIZE, O * V), (0.66 * (O * V * P_SIZE) ** (0 - 0.16667)), 0.4375, ((0, 16), (1, 16)))
    eps_occ = jnp.clip(-2.0 + 1.6 * jax.random.uniform(seeds[1], (NOCC,), jnp.float32) ** block_levels(seeds[1], (NOCC,), ((0, 16),), -0.2, 0.2), -2.0, -0.4)
    eps_vir = jnp.clip(jax.random.uniform(seeds[2], (V,), jnp.float32, 0.2, 2.5), 0.2, 2.5)
    pairs = draw_pairs(jax.random.fold_in(seeds[4], 71), 0)
    return dict(blocks=blocks, eps_occ=eps_occ, eps_vir=eps_vir, pairs=pairs)


def pair_terms(left_matrix, right_matrix, first_energy, second_energy, eps_vir):
    orbitals = first_energy.shape[0]
    virtuals = eps_vir.shape[0]
    width = orbitals * virtuals
    integrals = lax.dot_general(left_matrix, right_matrix, (((0,), (0,)), ((), ())), preferred_element_type=jnp.float32)
    gaps = (first_energy[:, None, None, None] + second_energy[None, None, :, None]
            - eps_vir[None, :, None, None] - eps_vir[None, None, None, :])
    amplitude = integrals.reshape(orbitals, virtuals, orbitals, virtuals) / gaps
    combined = (2.0 * amplitude - jnp.transpose(amplitude, (0, 3, 2, 1))).astype(jnp.bfloat16).reshape(width, width)
    first_grad = lax.dot_general(right_matrix, combined, (((1,), (1,)), ((), ())), preferred_element_type=jnp.float32)
    second_grad = jnp.dot(left_matrix, combined, preferred_element_type=jnp.float32)
    return first_grad, second_grad


def reference(blocks, eps_occ, eps_vir, pairs):
    orbitals = eps_occ.shape[0] // blocks.shape[0]
    gradient = jnp.zeros(blocks.shape, jnp.float32)

    def visit(number, totals):
        first_id = jnp.maximum(pairs[number, 0], 0).astype(jnp.int32)
        second_id = jnp.maximum(pairs[number, 1], 0).astype(jnp.int32)

        def work(current):
            first_rows = lax.dynamic_index_in_dim(blocks, first_id, 0, keepdims=False)
            second_rows = lax.dynamic_index_in_dim(blocks, second_id, 0, keepdims=False)
            first_energy = lax.dynamic_slice_in_dim(eps_occ, first_id * orbitals, orbitals)
            second_energy = lax.dynamic_slice_in_dim(eps_occ, second_id * orbitals, orbitals)
            first_grad, second_grad = pair_terms(first_rows, second_rows, first_energy, second_energy, eps_vir)
            current = current.at[first_id].add(first_grad)
            current = current.at[second_id].add(second_grad)
            return current

        def skip(current):
            return current

        return lax.cond(pairs[number, 0] >= 0, work, skip, totals)

    return lax.fori_loop(0, PAIRS, visit, gradient)
```

```python
import functools

import jax
import jax.numpy as jnp
from jax import lax
from jax.experimental import pallas as pl
from jax.experimental.pallas import tpu as pltpu
from jax.sharding import PartitionSpec as P

NONE = 7
OWN = (3, 4, 3, 4, 3, 4, 2, NONE, 0, 1, 5, 1, 1, 2, 0, 1)
SHARED = (0, 1, 2, NONE, 5, 2, 0, NONE)
COLS = 16
CHIPS = 8
ROWS = 56
SLOT = 64
ORB = 4
VIRT = 224
PAD = 256
WIDTH = ORB * VIRT
WIDE = ORB * PAD
FULL = COLS * SLOT
MESH = pl.DeviceIdType.MESH


def packed(table):
    return sum(value << (3 * place) for place, value in enumerate(table))


def own_of(c):
    low, high = packed(OWN[:8]), packed(OWN[8:])
    return (jnp.where(c < 8, low, high) >> (3 * (c % 8))) & 7


def shared_of(q):
    return (jnp.int32(packed(SHARED)) >> (3 * q)) & 7


def away(c, t):
    z, y, k = c // 8, (c // 2) % 4, c % 2
    dz, dy, dk = t // 8, (t // 2) % 4, t % 2
    return ((z + dz) % 2) * 8 + ((y + dy) % 4) * 2 + (k + dk) % 2


def kernel(
    blocks, eps, vir, pairs, out,
    nxt, energy, own_slots, shared_slots, y_wide, u_mat, ut_mat, gaps, alive,
    g_own, g_keep, g_give, g_sib, g_sum, r_own, r_shared, give_back, got_back,
    nxt_sem, own_send, own_recv, shared_send, shared_recv, hand_send,
    sib_send, sib_recv, term_send, term_recv, sum_send, sum_recv, back_send, back_recv,
):
    row = lax.axis_index("row")
    c = lax.axis_index("col")
    n_row = lax.axis_size("row")
    ahead, behind = (row + 1) % n_row, (row + n_row - 1) % n_row
    q, k = c // 2, c % 2
    sibling = q * 2 + 1 - k
    mine, common = own_of(c), shared_of(q)
    paired = common != NONE

    barrier = pltpu.get_barrier_semaphore()

    def greet(t, _):
        pl.semaphore_signal(barrier, inc=1, device_id={"col": away(c, t)}, device_id_type=MESH)
        return 0

    lax.fori_loop(1, COLS, greet, 0)
    for r in (ahead, behind):
        pl.semaphore_signal(barrier, inc=1, device_id={"row": r}, device_id_type=MESH)
    pl.semaphore_wait(barrier, COLS - 1 + 2)

    def remote(src, dst, send, recv, where):
        return pltpu.make_async_remote_copy(
            src_ref=src, dst_ref=dst, send_sem=send, recv_sem=recv, device_id=where, device_id_type=MESH
        )

    ship = remote(blocks, nxt, nxt_sem.at[0], nxt_sem.at[1], {"row": behind})
    ship_energy = remote(eps, energy.at[pl.ds(3, 3)], nxt_sem.at[2], nxt_sem.at[3], {"row": behind})
    ship.start()
    ship_energy.start()

    def own_copy(source, t, target, index):
        return remote(source.at[index], own_slots.at[c], own_send.at[t], own_recv.at[c], {"col": target})

    def shared_copy(source, t, target, index):
        return remote(source.at[index], shared_slots.at[c], shared_send.at[t], shared_recv.at[c], {"col": target})

    def send_blocks(source, first):
        def step(t, _):
            target = away(c, t)
            block = own_of(target)

            @pl.when((t > 0) & (block >= first) & (block < first + 3))
            def _():
                own_copy(source, t, target, block - first).start()

            block2 = shared_of(target // 2)

            @pl.when((t > 0) & (t % 2 == 0) & (block2 >= first) & (block2 < first + 3))
            def _():
                shared_copy(source, t // 2, target, block2 - first).start()

            return 0

        lax.fori_loop(0, COLS, step, 0)

        @pl.when((mine >= first) & (mine < first + 3))
        def _():
            own_slots[c] = source[mine - first]

        @pl.when((common >= first) & (common < first + 3))
        def _():
            shared_slots[c] = source[common - first]

    send_blocks(blocks, 0)

    y_wide[...] = jnp.zeros_like(y_wide)
    energy[pl.ds(0, 3)] = eps[...]
    virtual = jnp.broadcast_to(vir[...], (PAD, PAD))
    gaps[...] = virtual + virtual.T
    low, high = jnp.minimum(mine, common), jnp.where(common == NONE, mine, jnp.maximum(mine, common))
    first_id = row * 3 + low
    second_id = (row * 3 + high) % (n_row * 3)
    listed = pairs[...]
    hit = (listed[:, 0:1] == first_id) & (listed[:, 1:2] == second_id)
    alive[...] = jnp.broadcast_to(jnp.sum(jnp.where(hit, 1.0, 0.0), axis=0, keepdims=True), (8, 128))

    ship.wait_recv()
    send_blocks(nxt, 3)
    ship_energy.wait_recv()

    def unpack(which, slots, source):
        value = slots[source]
        at = pl.ds(pl.multiple_of(source * SLOT, SLOT), ROWS)
        for i in range(ORB):
            y_wide[which, at, pl.ds(i * PAD, VIRT)] = value[:, i * VIRT : (i + 1) * VIRT]

    def hand(source):
        return remote(
            shared_slots.at[source], shared_slots.at[source], hand_send.at[source // 2], shared_recv.at[source],
            {"col": sibling},
        )

    @pl.when(paired)
    def _():
        def step(t, _):
            source = away(c, 2 * t)

            @pl.when(t > 0)
            def _():
                hand(source).wait_recv()

            hand(source).start()
            unpack(1, shared_slots, source)
            return 0

        lax.fori_loop(0, CHIPS, step, 0)

    @pl.when(mine != NONE)
    def _():
        unpack(0, own_slots, c)

        def step(t, _):
            source = away(c, t)
            remote(blocks.at[0], own_slots.at[source], own_send.at[t], own_recv.at[source], {"col": source}).wait_recv()
            unpack(0, own_slots, source)
            return 0

        lax.fori_loop(1, COLS, step, 0)

    @pl.when(paired)
    def _():
        def step(t, _):
            source = away(sibling, 2 * t)
            hand(source).wait_recv()
            unpack(1, shared_slots, source)
            return 0

        lax.fori_loop(0, CHIPS, step, 0)

    partner = jnp.where(paired, 1, 0)
    mine_index = jnp.where(mine == NONE, 0, mine)
    common_index = jnp.where(paired, common, mine_index)

    def amplitudes(i, _):
        left = y_wide[0, :, pl.ds(pl.multiple_of(i * PAD, PAD), PAD)]
        at = pl.ds(pl.multiple_of(i * VIRT, 32), VIRT)
        energy_i = energy[mine_index, pl.ds(i, 1), :]
        energy_i = jnp.concatenate([energy_i, energy_i], axis=1)
        live = alive[0:1, 0:1]
        for j in range(ORB):
            right = y_wide[partner, :, j * PAD : (j + 1) * PAD]
            integrals = lax.dot_general(left, right, (((0,), (0,)), ((), ())), preferred_element_type=jnp.float32)
            energy_j = energy[common_index, j : j + 1, :]
            energy_j = jnp.concatenate([energy_j, energy_j], axis=1)
            amplitude = live * integrals / ((energy_i + energy_j) - gaps[...])
            flipped = amplitude.T
            u_mat[at, j * PAD : (j + 1) * PAD] = (2.0 * amplitude - flipped)[:VIRT].astype(jnp.bfloat16)
            ut_mat[j * VIRT : (j + 1) * VIRT, pl.ds(pl.multiple_of(i * PAD, PAD), PAD)] = (
                (2.0 * flipped - amplitude)[:VIRT].astype(jnp.bfloat16)
            )
        return 0

    lax.fori_loop(0, ORB, amplitudes, 0)

    def term_copy(target):
        return remote(g_own.at[target], r_own.at[c], term_send.at[target], term_recv.at[c], {"col": target})

    def sib_copy(chip):
        return remote(g_give.at[chip], g_sib.at[chip], sib_send.at[chip], sib_recv.at[chip], {"col": sibling})

    def sum_copy(chip):
        return remote(g_sum.at[chip], r_shared.at[q], sum_send.at[chip], sum_recv.at[q], {"col": chip * 2 + k})

    def part_of(step):
        return (c // 4 + 1 + step) % 4

    def add_shared(step):
        for h in range(2):
            chip = part_of(step) * 2 + h
            sib_copy(chip).wait_recv()
            total = (g_keep[chip] + g_sib[chip].astype(jnp.float32)).astype(jnp.bfloat16)
            g_sum[chip] = total

            @pl.when(chip != q)
            def _():
                sum_copy(chip).start()

            @pl.when(chip == q)
            def _():
                r_shared[q] = total

    def terms(step, _):
        part = part_of(step)
        at = pl.ds(pl.multiple_of(part * PAD, PAD), PAD)
        dims = (((1,), (1,)), ((), ()))
        to_shared = lax.dot_general(y_wide[0, at, :], ut_mat[...], dims, preferred_element_type=jnp.float32)

        @pl.when(paired)
        def _():
            for h in range(2):
                chip = part * 2 + h
                even = to_shared[2 * h * SLOT : 2 * h * SLOT + ROWS]
                odd = to_shared[(2 * h + 1) * SLOT : (2 * h + 1) * SLOT + ROWS]
                g_keep[chip] = jnp.where(k == 0, even, odd)
                g_give[chip] = jnp.where(k == 0, odd, even).astype(jnp.bfloat16)
                sib_copy(chip).start()

        to_own = lax.dot_general(y_wide[partner, at, :], u_mat[...], dims, preferred_element_type=jnp.float32)
        to_own = to_own + jnp.where(paired, 0.0, 1.0) * to_shared
        for n in range(4):
            target = part * 4 + n
            value = to_own[n * SLOT : n * SLOT + ROWS].astype(jnp.bfloat16)
            g_own[target] = value

            @pl.when((target != c) & (mine != NONE))
            def _():
                term_copy(target).start()

            @pl.when(target == c)
            def _():
                r_own[c] = value

        @pl.when(paired & (step > 0))
        def _():
            add_shared(step - 1)

        return 0

    lax.fori_loop(0, 4, terms, 0)

    @pl.when(paired)
    def _():
        add_shared(3)

    def total_of(block):
        total = jnp.zeros((ROWS, WIDTH), jnp.float32)
        for source in range(COLS):
            if OWN[source] == block:
                @pl.when(c != source)
                def _():
                    remote(
                        g_own.at[0], r_own.at[source], term_send.at[0], term_recv.at[source], {"col": sibling}
                    ).wait_recv()

                total = total + r_own[source].astype(jnp.float32)
        for chip in range(CHIPS):
            if SHARED[chip] == block:
                @pl.when(q != chip)
                def _():
                    remote(
                        g_sum.at[0], r_shared.at[chip], sum_send.at[0], sum_recv.at[chip], {"col": sibling}
                    ).wait_recv()

                total = total + r_shared[chip].astype(jnp.float32)
        return total

    def back_copy(index):
        return remote(
            give_back.at[index], got_back.at[index], back_send.at[index], back_recv.at[index], {"row": ahead}
        )

    for index in range(3):
        give_back[index] = total_of(3 + index).astype(jnp.bfloat16)
        back_copy(index).start()
    for index in range(3):
        total = total_of(index)
        back_copy(index).wait_recv()
        out[index] = total + got_back[index].astype(jnp.float32)

    ship.wait_send()
    ship_energy.wait_send()
    for index in range(3):
        back_copy(index).wait_send()

    def drain(t, _):
        target = away(c, t)

        @pl.when((t > 0) & (own_of(target) != NONE))
        def _():
            own_copy(blocks, t, target, 0).wait_send()

        @pl.when((t > 0) & (t % 2 == 0) & (shared_of(target // 2) != NONE))
        def _():
            shared_copy(blocks, t // 2, target, 0).wait_send()

        @pl.when((t > 0) & (mine != NONE))
        def _():
            term_copy(target).wait_send()

        return 0

    lax.fori_loop(0, COLS, drain, 0)

    @pl.when(paired)
    def _():
        def drain_chip(t, _):
            hand(away(c, 2 * t)).wait_send()
            sib_copy(t).wait_send()

            @pl.when(t != q)
            def _():
                sum_copy(t).wait_send()

            return 0

        lax.fori_loop(0, CHIPS, drain_chip, 0)


def body(blocks, eps_occ, eps_vir, pairs):
    eps = jnp.broadcast_to(eps_occ.reshape(3, ORB, 1), (3, ORB, 128))
    vir = jnp.pad(eps_vir, (0, PAD - VIRT)).reshape(1, PAD)
    vmem = pl.BlockSpec(memory_space=pltpu.VMEM)
    bf16, f32 = jnp.bfloat16, jnp.float32
    dma = pltpu.SemaphoreType.DMA
    slab = (ROWS, WIDTH)
    return pl.pallas_call(
        kernel,
        out_shape=jax.ShapeDtypeStruct(blocks.shape, f32),
        in_specs=[vmem] * 4,
        out_specs=vmem,
        scratch_shapes=[
            pltpu.VMEM((3,) + slab, bf16),
            pltpu.VMEM((6, ORB, 128), f32),
            pltpu.VMEM((COLS,) + slab, bf16),
            pltpu.VMEM((COLS,) + slab, bf16),
            pltpu.VMEM((2, FULL, WIDE), bf16),
            pltpu.VMEM((WIDTH, WIDE), bf16),
            pltpu.VMEM((WIDTH, WIDE), bf16),
            pltpu.VMEM((PAD, PAD), f32),
            pltpu.VMEM((8, 128), f32),
            pltpu.VMEM((COLS,) + slab, bf16),
            pltpu.VMEM((CHIPS,) + slab, f32),
            pltpu.VMEM((CHIPS,) + slab, bf16),
            pltpu.VMEM((CHIPS,) + slab, bf16),
            pltpu.VMEM((CHIPS,) + slab, bf16),
            pltpu.VMEM((COLS,) + slab, bf16),
            pltpu.VMEM((CHIPS,) + slab, bf16),
            pltpu.VMEM((3,) + slab, bf16),
            pltpu.VMEM((3,) + slab, bf16),
            dma((4,)),
            dma((COLS,)), dma((COLS,)), dma((CHIPS,)), dma((COLS,)), dma((CHIPS,)),
            dma((CHIPS,)), dma((CHIPS,)), dma((COLS,)), dma((COLS,)), dma((CHIPS,)), dma((CHIPS,)),
            dma((3,)), dma((3,)),
        ],
        compiler_params=pltpu.CompilerParams(
            collective_id=0, has_side_effects=True, vmem_limit_bytes=48 * 1024 * 1024
        ),
        cost_estimate=pl.CostEstimate(flops=6 * FULL**3, bytes_accessed=4 * 1024 * 1024, transcendentals=0),
    )(blocks, eps, vir, pairs)


def solution(mesh):
    in_specs = (P("row", "col", None), P("row"), P(), P("row", None))
    out_specs = P("row", "col", None)
    return jax.shard_map(body, mesh=mesh, in_specs=in_specs, out_specs=out_specs, check_vma=False)
```

```python
import functools

import jax
import jax.numpy as jnp
from jax import lax
from jax.experimental import pallas as pl
from jax.experimental.pallas import tpu as pltpu
from jax.sharding import PartitionSpec as P

NONE = 7
OWN = (0, 1, 5, 1, 1, 2, 0, 1, 3, 4, 3, 4, 3, 4, 2, NONE)
SHARED = (5, 2, 0, NONE, 0, 1, 2, NONE)
NEXT = ((5,), (3, 4))
PLANE = 8
RING = 4
COLS = 16
CHIPS = 8
ROWS = 56
SLOT = 64
ORB = 4
VIRT = 224
PAD = 256
WIDTH = ORB * VIRT
WIDE = ORB * PAD
FULL = COLS * SLOT
MESH = pl.DeviceIdType.MESH


def packed(table):
    return sum(value << (3 * place) for place, value in enumerate(table))


def own_of(c):
    low, high = packed(OWN[:8]), packed(OWN[8:])
    return (jnp.where(c < 8, low, high) >> (3 * (c % 8))) & 7


def shared_of(q):
    return (jnp.int32(packed(SHARED)) >> (3 * q)) & 7


def kernel(
    blocks, eps, vir, pairs, out,
    across, nxt, energy, own_slots, shared_slots, y_wide, u_mat, ut_mat, gaps, alive,
    g_own, g_keep, g_give, g_sib, g_sum, r_own, r_shared, give_back, got_back, give_across, got_across,
    energy_sem, across_send, across_recv, next_send, next_recv,
    own_send, own_recv, shared_send, shared_recv, hand_send,
    sib_send, sib_recv, term_send, term_recv, sum_send, sum_recv, back_send, back_recv, cross_send, cross_recv,
):
    row = lax.axis_index("row")
    c = lax.axis_index("col")
    n_row = lax.axis_size("row")
    ahead, behind = (row + 1) % n_row, (row + n_row - 1) % n_row
    z, y, k = c // PLANE, (c // 2) % RING, c % 2
    q, here = c // 2, c % PLANE
    sibling = q * 2 + 1 - k
    partner_z = (1 - z) * PLANE + here
    mine, common = own_of(c), shared_of(q)
    paired = common != NONE

    def place(t):
        return ((y + t // 2) % RING) * 2 + (k + t % 2) % 2

    barrier = pltpu.get_barrier_semaphore()

    def greet(t, _):
        pl.semaphore_signal(barrier, inc=1, device_id={"col": z * PLANE + place(t)}, device_id_type=MESH)
        return 0

    for r in (behind, ahead):
        for half in range(2):
            pl.semaphore_signal(
                barrier, inc=1, device_id={"row": r, "col": half * PLANE + here}, device_id_type=MESH
            )
    pl.semaphore_signal(barrier, inc=1, device_id={"col": partner_z}, device_id_type=MESH)
    lax.fori_loop(1, PLANE, greet, 0)
    pl.semaphore_wait(barrier, PLANE - 1 + 1 + 4)

    def remote(src, dst, send, recv, where):
        return pltpu.make_async_remote_copy(
            src_ref=src, dst_ref=dst, send_sem=send, recv_sem=recv, device_id=where, device_id_type=MESH
        )

    def ship(index, half, source_half):
        return remote(
            blocks.at[index], nxt.at[source_half, index], next_send.at[index], next_recv.at[source_half * 3 + index],
            {"row": behind, "col": half * PLANE + here},
        )

    def cross(index):
        return remote(
            blocks.at[index], across.at[index], across_send.at[index], across_recv.at[index], {"col": partner_z}
        )

    ship_energy = remote(eps, energy.at[pl.ds(3, 3)], energy_sem.at[0], energy_sem.at[1], {"row": behind})
    for half in (1, 0):
        for block in NEXT[half]:
            ship(block - 3, half, z).start()
    for index in range(3):
        cross(index).start()
    ship_energy.start()

    def own_copy(source, far, t, index):
        slot = ((z + far) % 2) * PLANE + here
        return remote(
            source.at[index], own_slots.at[slot], own_send.at[far * PLANE + t], own_recv.at[slot],
            {"col": z * PLANE + place(t)},
        )

    def shared_copy(source, far, t, index):
        slot = ((z + far) % 2) * PLANE + here
        return remote(
            source.at[index], shared_slots.at[slot], shared_send.at[far * RING + t // 2], shared_recv.at[slot],
            {"col": z * PLANE + place(t)},
        )

    def send_blocks(source, far, first):
        def step(t, _):
            target = z * PLANE + place(t)
            block = own_of(target)

            @pl.when((block >= first) & (block < first + 3))
            def _():
                own_copy(source, far, t, block - first).start()

            block2 = shared_of(target // 2)

            @pl.when((t % 2 == 0) & (block2 >= first) & (block2 < first + 3))
            def _():
                shared_copy(source, far, t, block2 - first).start()

            return 0

        lax.fori_loop(1, PLANE, step, 0)
        slot = ((z + far) % 2) * PLANE + here

        @pl.when((mine >= first) & (mine < first + 3))
        def _():
            own_slots[slot] = source[mine - first]

        @pl.when((common >= first) & (common < first + 3))
        def _():
            shared_slots[slot] = source[common - first]

    send_blocks(blocks, 0, 0)

    y_wide[...] = jnp.zeros_like(y_wide)
    energy[pl.ds(0, 3)] = eps[...]
    virtual = jnp.broadcast_to(vir[...], (PAD, PAD))
    gaps[...] = virtual + virtual.T
    low, high = jnp.minimum(mine, common), jnp.where(common == NONE, mine, jnp.maximum(mine, common))
    first_id = row * 3 + low
    second_id = (row * 3 + high) % (n_row * 3)
    listed = pairs[...]
    hit = (listed[:, 0:1] == first_id) & (listed[:, 1:2] == second_id)
    alive[...] = jnp.broadcast_to(jnp.sum(jnp.where(hit, 1.0, 0.0), axis=0, keepdims=True), (8, 128))

    for index in range(3):
        cross(index).wait_recv()
    send_blocks(across, 1, 0)

    for far in range(2):
        source_half = (z + far) % 2
        for half in range(2):
            @pl.when(z == half)
            def _():
                for block in NEXT[half]:
                    ship(block - 3, half, source_half).wait_recv()

        send_blocks(nxt.at[source_half], far, 3)
    ship_energy.wait_recv()

    def unpack(which, slots, source):
        value = slots[source]
        at = pl.ds(pl.multiple_of(source * SLOT, SLOT), ROWS)
        for i in range(ORB):
            y_wide[which, at, pl.ds(i * PAD, VIRT)] = value[:, i * VIRT : (i + 1) * VIRT]

    def hand(source):
        return remote(
            shared_slots.at[source], shared_slots.at[source], hand_send.at[source // 2], shared_recv.at[source],
            {"col": sibling},
        )

    @pl.when(paired)
    def _():
        def step(t, _):
            source = ((z + t // RING) % 2) * PLANE + ((y + t) % RING) * 2 + k

            @pl.when(t % RING > 0)
            def _():
                hand(source).wait_recv()

            hand(source).start()
            unpack(1, shared_slots, source)
            return 0

        lax.fori_loop(0, CHIPS, step, 0)

    @pl.when(mine != NONE)
    def _():
        def step(t, _):
            source = ((z + t // PLANE) % 2) * PLANE + place(t % PLANE)

            @pl.when(t % PLANE > 0)
            def _():
                remote(
                    blocks.at[0], own_slots.at[source], own_send.at[t], own_recv.at[source], {"col": sibling}
                ).wait_recv()

            unpack(0, own_slots, source)
            return 0

        lax.fori_loop(0, COLS, step, 0)

    @pl.when(paired)
    def _():
        def step(t, _):
            source = ((z + t // RING) % 2) * PLANE + ((y + t) % RING) * 2 + 1 - k
            hand(source).wait_recv()
            unpack(1, shared_slots, source)
            return 0

        lax.fori_loop(0, CHIPS, step, 0)

    partner = jnp.where(paired, 1, 0)
    mine_index = jnp.where(mine == NONE, 0, mine)
    common_index = jnp.where(paired, common, mine_index)

    def amplitudes(i, _):
        left = y_wide[0, :, pl.ds(pl.multiple_of(i * PAD, PAD), PAD)]
        at = pl.ds(pl.multiple_of(i * VIRT, 32), VIRT)
        energy_i = energy[mine_index, pl.ds(i, 1), :]
        energy_i = jnp.concatenate([energy_i, energy_i], axis=1)
        live = alive[0:1, 0:1]
        for j in range(ORB):
            right = y_wide[partner, :, j * PAD : (j + 1) * PAD]
            integrals = lax.dot_general(left, right, (((0,), (0,)), ((), ())), preferred_element_type=jnp.float32)
            energy_j = energy[common_index, j : j + 1, :]
            energy_j = jnp.concatenate([energy_j, energy_j], axis=1)
            amplitude = live * integrals / ((energy_i + energy_j) - gaps[...])
            flipped = amplitude.T
            u_mat[at, j * PAD : (j + 1) * PAD] = (2.0 * amplitude - flipped)[:VIRT].astype(jnp.bfloat16)
            ut_mat[j * VIRT : (j + 1) * VIRT, pl.ds(pl.multiple_of(i * PAD, PAD), PAD)] = (
                (2.0 * flipped - amplitude)[:VIRT].astype(jnp.bfloat16)
            )
        return 0

    lax.fori_loop(0, ORB, amplitudes, 0)

    def term_copy(s):
        return remote(
            g_own.at[s], r_own.at[(s // PLANE) * PLANE + here], term_send.at[s],
            term_recv.at[(s // PLANE) * PLANE + here], {"col": z * PLANE + s % PLANE},
        )

    def sib_copy(chip):
        return remote(g_give.at[chip], g_sib.at[chip], sib_send.at[chip], sib_recv.at[chip], {"col": sibling})

    def sum_copy(chip):
        at = (chip // RING) * RING + y
        return remote(
            g_sum.at[chip], r_shared.at[at], sum_send.at[chip], sum_recv.at[at],
            {"col": z * PLANE + (chip % RING) * 2 + k},
        )

    def part_of(step):
        return ((z + 1 + step // 2) % 2) * 2 + (y // 2 + 1 + step) % 2

    def add_shared(step):
        for h in range(2):
            chip = part_of(step) * 2 + h
            sib_copy(chip).wait_recv()
            total = (g_keep[chip] + g_sib[chip].astype(jnp.float32)).astype(jnp.bfloat16)
            g_sum[chip] = total

            @pl.when(chip % RING != y)
            def _():
                sum_copy(chip).start()

            @pl.when(chip % RING == y)
            def _():
                r_shared[chip] = total

    def terms(step, _):
        part = part_of(step)
        at = pl.ds(pl.multiple_of(part * PAD, PAD), PAD)
        dims = (((1,), (1,)), ((), ()))
        to_shared = lax.dot_general(y_wide[0, at, :], ut_mat[...], dims, preferred_element_type=jnp.float32)

        @pl.when(paired)
        def _():
            for h in range(2):
                chip = part * 2 + h
                even = to_shared[2 * h * SLOT : 2 * h * SLOT + ROWS]
                odd = to_shared[(2 * h + 1) * SLOT : (2 * h + 1) * SLOT + ROWS]
                g_keep[chip] = jnp.where(k == 0, even, odd)
                g_give[chip] = jnp.where(k == 0, odd, even).astype(jnp.bfloat16)
                sib_copy(chip).start()

        to_own = lax.dot_general(y_wide[partner, at, :], u_mat[...], dims, preferred_element_type=jnp.float32)
        to_own = to_own + jnp.where(paired, 0.0, 1.0) * to_shared
        for n in range(4):
            target = part * 4 + n
            value = to_own[n * SLOT : n * SLOT + ROWS].astype(jnp.bfloat16)
            g_own[target] = value

            @pl.when((target % PLANE != here) & (mine != NONE))
            def _():
                term_copy(target).start()

            @pl.when(target % PLANE == here)
            def _():
                r_own[target] = value

        @pl.when(paired & (step > 0))
        def _():
            add_shared(step - 1)

        return 0

    lax.fori_loop(0, 4, terms, 0)

    @pl.when(paired)
    def _():
        add_shared(3)

    def total_of(half, at, block):
        total = jnp.zeros((ROWS, WIDTH), jnp.float32)
        for source in range(PLANE):
            if OWN[half * PLANE + source] == block:
                @pl.when(here != source)
                def _():
                    remote(
                        g_own.at[0], r_own.at[at * PLANE + source], term_send.at[0],
                        term_recv.at[at * PLANE + source], {"col": sibling},
                    ).wait_recv()

                total = total + r_own[at * PLANE + source].astype(jnp.float32)
        for chip in range(RING):
            if SHARED[half * RING + chip] == block:
                @pl.when(y != chip)
                def _():
                    remote(
                        g_sum.at[0], r_shared.at[at * RING + chip], sum_send.at[0],
                        sum_recv.at[at * RING + chip], {"col": sibling},
                    ).wait_recv()

                total = total + r_shared[at * RING + chip].astype(jnp.float32)
        return total

    def back_copy(index, at):
        return remote(
            give_back.at[at, index], got_back.at[index], back_send.at[at * 3 + index], back_recv.at[index],
            {"row": ahead, "col": at * PLANE + here},
        )

    def cross_copy(index):
        return remote(
            give_across.at[index], got_across.at[index], cross_send.at[index], cross_recv.at[index],
            {"col": partner_z},
        )

    for half in range(2):
        @pl.when(z == half)
        def _():
            for at in (1 - half, half):
                for block in NEXT[half]:
                    give_back[at, block - 3] = total_of(half, at, block).astype(jnp.bfloat16)
                    back_copy(block - 3, at).start()
                for index in range(3):
                    total = total_of(half, at, index)
                    if at == half:
                        out[index] = total
                    else:
                        give_across[index] = total.astype(jnp.bfloat16)
                        cross_copy(index).start()

    for index in range(3):
        cross_copy(index).wait_recv()
        back_copy(index, 0).wait_recv()
        out[index] += got_across[index].astype(jnp.float32) + got_back[index].astype(jnp.float32)

    ship_energy.wait_send()
    for index in range(3):
        cross(index).wait_send()
        ship(index, 0, 0).wait_send()
        cross_copy(index).wait_send()
    for half in range(2):
        @pl.when(z == half)
        def _():
            for at in range(2):
                for block in NEXT[half]:
                    back_copy(block - 3, at).wait_send()

    def drain(n, _):
        far, t = n // PLANE, n % PLANE
        target = z * PLANE + place(t)

        @pl.when((t > 0) & (own_of(target) != NONE))
        def _():
            own_copy(blocks, far, t, 0).wait_send()

        @pl.when((t > 0) & (t % 2 == 0) & (shared_of(target // 2) != NONE))
        def _():
            shared_copy(blocks, far, t, 0).wait_send()

        @pl.when((n % PLANE != here) & (mine != NONE))
        def _():
            term_copy(n).wait_send()

        return 0

    lax.fori_loop(0, COLS, drain, 0)

    @pl.when(paired)
    def _():
        def drain_chip(chip, _):
            hand(chip * 2 + k).wait_send()
            sib_copy(chip).wait_send()

            @pl.when(chip % RING != y)
            def _():
                sum_copy(chip).wait_send()

            return 0

        lax.fori_loop(0, CHIPS, drain_chip, 0)


def body(blocks, eps_occ, eps_vir, pairs):
    eps = jnp.broadcast_to(eps_occ.reshape(3, ORB, 1), (3, ORB, 128))
    vir = jnp.pad(eps_vir, (0, PAD - VIRT)).reshape(1, PAD)
    vmem = pl.BlockSpec(memory_space=pltpu.VMEM)
    bf16, f32 = jnp.bfloat16, jnp.float32
    dma = pltpu.SemaphoreType.DMA
    slab = (ROWS, WIDTH)
    return pl.pallas_call(
        kernel,
        out_shape=jax.ShapeDtypeStruct(blocks.shape, f32),
        in_specs=[vmem] * 4,
        out_specs=vmem,
        scratch_shapes=[
            pltpu.VMEM((3,) + slab, bf16),
            pltpu.VMEM((2, 3) + slab, bf16),
            pltpu.VMEM((6, ORB, 128), f32),
            pltpu.VMEM((COLS,) + slab, bf16),
            pltpu.VMEM((COLS,) + slab, bf16),
            pltpu.VMEM((2, FULL, WIDE), bf16),
            pltpu.VMEM((WIDTH, WIDE), bf16),
            pltpu.VMEM((WIDTH, WIDE), bf16),
            pltpu.VMEM((PAD, PAD), f32),
            pltpu.VMEM((8, 128), f32),
            pltpu.VMEM((COLS,) + slab, bf16),
            pltpu.VMEM((CHIPS,) + slab, f32),
            pltpu.VMEM((CHIPS,) + slab, bf16),
            pltpu.VMEM((CHIPS,) + slab, bf16),
            pltpu.VMEM((CHIPS,) + slab, bf16),
            pltpu.VMEM((COLS,) + slab, bf16),
            pltpu.VMEM((CHIPS,) + slab, bf16),
            pltpu.VMEM((2, 3) + slab, bf16),
            pltpu.VMEM((3,) + slab, bf16),
            pltpu.VMEM((3,) + slab, bf16),
            pltpu.VMEM((3,) + slab, bf16),
            dma((2,)), dma((3,)), dma((3,)), dma((3,)), dma((6,)),
            dma((COLS,)), dma((COLS,)), dma((CHIPS,)), dma((COLS,)), dma((CHIPS,)),
            dma((CHIPS,)), dma((CHIPS,)), dma((COLS,)), dma((COLS,)), dma((CHIPS,)), dma((CHIPS,)),
            dma((6,)), dma((3,)), dma((3,)), dma((3,)),
        ],
        compiler_params=pltpu.CompilerParams(
            collective_id=0, has_side_effects=True, vmem_limit_bytes=48 * 1024 * 1024
        ),
        cost_estimate=pl.CostEstimate(flops=6 * FULL**3, bytes_accessed=4 * 1024 * 1024, transcendentals=0),
    )(blocks, eps, vir, pairs)


def solution(mesh):
    in_specs = (P("row", "col", None), P("row"), P(), P("row", None))
    out_specs = P("row", "col", None)
    return jax.shard_map(body, mesh=mesh, in_specs=in_specs, out_specs=out_specs, check_vma=False)
```

```python
import functools

import jax
import jax.numpy as jnp
from jax import lax
from jax.experimental import pallas as pl
from jax.experimental.pallas import tpu as pltpu
from jax.sharding import PartitionSpec as P

NONE = 7
OWN = (0, 1, 1, 2, 5, 1, 0, 1, 0, 1, 0, 1, 3, 4, 2, NONE)
SHARED = (5, 0, 2, NONE, 3, 4, 2, NONE)
NEXT = ((5,), (3, 4))
PLANE = 8
RING = 4
COLS = 16
CHIPS = 8
ROWS = 56
SLOT = 64
ORB = 4
VIRT = 224
PAD = 256
WIDTH = ORB * VIRT
WIDE = ORB * PAD
FULL = COLS * SLOT
MESH = pl.DeviceIdType.MESH


def packed(table):
    return sum(value << (3 * place) for place, value in enumerate(table))


def own_of(c):
    low, high = packed(OWN[:8]), packed(OWN[8:])
    return (jnp.where(c < 8, low, high) >> (3 * (c % 8))) & 7


def shared_of(q):
    return (jnp.int32(packed(SHARED)) >> (3 * q)) & 7


def kernel(
    blocks_in, eps_in, vir_in, pairs_in, out,
    blocks, levels, vir, pairs, fetch_sem,
    across, nxt, energy, virtual_row, own_slots, shared_slots, y_wide, u_mat, ut_mat, gaps, alive,
    g_own, g_keep, g_give, g_sib, g_sum, r_own, r_shared, give_back, got_back, give_across, got_across,
    energy_sem, across_send, across_recv, next_send, next_recv,
    own_send, own_recv, shared_send, shared_recv, hand_send,
    sib_send, sib_recv, term_send, term_recv, sum_send, sum_recv, back_send, back_recv, cross_send, cross_recv,
):
    row = lax.axis_index("row")
    c = lax.axis_index("col")
    n_row = lax.axis_size("row")
    ahead, behind = (row + 1) % n_row, (row + n_row - 1) % n_row
    z, y, k = c // PLANE, (c // 2) % RING, c % 2
    q, here = c // 2, c % PLANE
    sibling = q * 2 + 1 - k
    partner_z = (1 - z) * PLANE + here
    mine, common = own_of(c), shared_of(q)
    paired = common != NONE

    def place(t):
        return ((y + t // 2) % RING) * 2 + (k + t % 2) % 2

    fetches = [
        pltpu.make_async_copy(source, target, fetch_sem.at[n])
        for n, (source, target) in enumerate(
            ((blocks_in, blocks), (eps_in, levels.at[0]), (vir_in, vir), (pairs_in, pairs))
        )
    ]
    for fetch in fetches:
        fetch.start()
    barrier = pltpu.get_barrier_semaphore()

    def greet(t, _):
        pl.semaphore_signal(barrier, inc=1, device_id={"col": z * PLANE + place(t)}, device_id_type=MESH)
        return 0

    for r in (behind, ahead):
        for half in range(2):
            pl.semaphore_signal(
                barrier, inc=1, device_id={"row": r, "col": half * PLANE + here}, device_id_type=MESH
            )
    pl.semaphore_signal(barrier, inc=1, device_id={"col": partner_z}, device_id_type=MESH)
    lax.fori_loop(1, PLANE, greet, 0)
    pl.semaphore_wait(barrier, PLANE - 1 + 1 + 4)
    for fetch in fetches:
        fetch.wait()

    def remote(src, dst, send, recv, where):
        return pltpu.make_async_remote_copy(
            src_ref=src, dst_ref=dst, send_sem=send, recv_sem=recv, device_id=where, device_id_type=MESH
        )

    def ship(index, half, source_half):
        return remote(
            blocks.at[index], nxt.at[source_half, index], next_send.at[index], next_recv.at[source_half * 3 + index],
            {"row": behind, "col": half * PLANE + here},
        )

    def cross(index):
        return remote(
            blocks.at[index], across.at[index], across_send.at[index], across_recv.at[index], {"col": partner_z}
        )

    ship_energy = remote(levels.at[0], levels.at[1], energy_sem.at[0], energy_sem.at[1], {"row": behind})
    for index in range(3):
        cross(index).start()
    for half in (1, 0):
        for block in NEXT[half]:
            ship(block - 3, half, z).start()
    ship_energy.start()

    def own_copy(source, far, t, index):
        slot = ((z + far) % 2) * PLANE + here
        return remote(
            source.at[index], own_slots.at[slot], own_send.at[far * PLANE + t], own_recv.at[slot],
            {"col": z * PLANE + place(t)},
        )

    def shared_copy(source, far, t, index):
        slot = ((z + far) % 2) * PLANE + here
        return remote(
            source.at[index], shared_slots.at[slot], shared_send.at[far * RING + t // 2], shared_recv.at[slot],
            {"col": z * PLANE + place(t)},
        )

    def send_blocks(source, far, first):
        def step(t, _):
            target = z * PLANE + place(t)
            block = own_of(target)

            @pl.when((block >= first) & (block < first + 3))
            def _():
                own_copy(source, far, t, block - first).start()

            block2 = shared_of(target // 2)

            @pl.when((t % 2 == 0) & (block2 >= first) & (block2 < first + 3))
            def _():
                shared_copy(source, far, t, block2 - first).start()

            return 0

        lax.fori_loop(1, PLANE, step, 0)
        slot = ((z + far) % 2) * PLANE + here

        @pl.when((mine >= first) & (mine < first + 3))
        def _():
            own_slots[slot] = source[mine - first]

        @pl.when((common >= first) & (common < first + 3))
        def _():
            shared_slots[slot] = source[common - first]

    send_blocks(blocks, 0, 0)

    y_wide[...] = jnp.zeros_like(y_wide)
    virtual_row[...] = jnp.zeros_like(virtual_row)
    virtual_row[:, 0:VIRT] = vir[...]
    virtual = jnp.broadcast_to(virtual_row[...], (PAD, PAD))
    gaps[...] = virtual + virtual.T
    low, high = jnp.minimum(mine, common), jnp.where(common == NONE, mine, jnp.maximum(mine, common))
    first_id = row * 3 + low
    second_id = (row * 3 + high) % (n_row * 3)
    hit = (pairs[0:1, :] == first_id) & (pairs[1:2, :] == second_id)
    alive[...] = jnp.broadcast_to(jnp.sum(jnp.where(hit, 1.0, 0.0), axis=1, keepdims=True), (8, 128))

    for index in range(3):
        cross(index).wait_recv()
    send_blocks(across, 1, 0)

    for far in range(2):
        source_half = (z + far) % 2
        for half in range(2):
            @pl.when(z == half)
            def _():
                for block in NEXT[half]:
                    ship(block - 3, half, source_half).wait_recv()

        send_blocks(nxt.at[source_half], far, 3)
    ship_energy.wait_recv()

    def unpack(which, slots, source):
        value = slots[source]
        at = pl.ds(pl.multiple_of(source * SLOT, SLOT), ROWS)
        for i in range(ORB):
            y_wide[which, at, pl.ds(i * PAD, VIRT)] = value[:, i * VIRT : (i + 1) * VIRT]

    def hand(source):
        return remote(
            shared_slots.at[source], shared_slots.at[source], hand_send.at[source // 2], shared_recv.at[source],
            {"col": sibling},
        )

    @pl.when(paired)
    def _():
        def step(t, _):
            source = ((z + t // RING) % 2) * PLANE + ((y + t) % RING) * 2 + k

            @pl.when(t % RING > 0)
            def _():
                hand(source).wait_recv()

            hand(source).start()
            unpack(1, shared_slots, source)
            return 0

        lax.fori_loop(0, CHIPS, step, 0)

    @pl.when(mine != NONE)
    def _():
        def step(t, _):
            source = ((z + t // PLANE) % 2) * PLANE + place(t % PLANE)

            @pl.when(t % PLANE > 0)
            def _():
                remote(
                    blocks.at[0], own_slots.at[source], own_send.at[t], own_recv.at[source], {"col": sibling}
                ).wait_recv()

            unpack(0, own_slots, source)
            return 0

        lax.fori_loop(0, COLS, step, 0)

    @pl.when(paired)
    def _():
        def step(t, _):
            source = ((z + t // RING) % 2) * PLANE + ((y + t) % RING) * 2 + 1 - k
            hand(source).wait_recv()
            unpack(1, shared_slots, source)
            return 0

        lax.fori_loop(0, CHIPS, step, 0)

    partner = jnp.where(paired, 1, 0)
    mine_index = jnp.where(mine == NONE, 0, mine)
    common_index = jnp.where(paired, common, mine_index)
    lane = lax.broadcasted_iota(jnp.int32, (1, 3 * ORB), 1)
    for which, index in enumerate((mine_index, common_index)):
        held = levels[index // 3]
        for i in range(ORB):
            level = jnp.sum(jnp.where(lane == (index % 3) * ORB + i, held, 0.0), axis=1, keepdims=True)
            energy[which, i : i + 1, :] = jnp.broadcast_to(level, (1, PAD))

    def amplitudes(i, _):
        left = y_wide[0, :, pl.ds(pl.multiple_of(i * PAD, PAD), PAD)]
        at = pl.ds(pl.multiple_of(i * VIRT, 32), VIRT)
        energy_i = energy[0, pl.ds(i, 1), :]
        live = alive[0:1, 0:1]
        for j in range(ORB):
            right = y_wide[partner, :, j * PAD : (j + 1) * PAD]
            integrals = lax.dot_general(left, right, (((0,), (0,)), ((), ())), preferred_element_type=jnp.float32)
            energy_j = energy[1, j : j + 1, :]
            amplitude = live * integrals / ((energy_i + energy_j) - gaps[...])
            flipped = amplitude.T
            u_mat[at, j * PAD : (j + 1) * PAD] = (2.0 * amplitude - flipped)[:VIRT].astype(jnp.bfloat16)
            ut_mat[j * VIRT : (j + 1) * VIRT, pl.ds(pl.multiple_of(i * PAD, PAD), PAD)] = (
                (2.0 * flipped - amplitude)[:VIRT].astype(jnp.bfloat16)
            )
        return 0

    lax.fori_loop(0, ORB, amplitudes, 0)

    def term_copy(s):
        return remote(
            g_own.at[s], r_own.at[(s // PLANE) * PLANE + here], term_send.at[s],
            term_recv.at[(s // PLANE) * PLANE + here], {"col": z * PLANE + s % PLANE},
        )

    def sib_copy(chip):
        return remote(g_give.at[chip], g_sib.at[chip], sib_send.at[chip], sib_recv.at[chip], {"col": sibling})

    def sum_copy(chip):
        at = (chip // RING) * RING + y
        return remote(
            g_sum.at[chip], r_shared.at[at], sum_send.at[chip], sum_recv.at[at],
            {"col": z * PLANE + (chip % RING) * 2 + k},
        )

    def part_of(step):
        return ((z + 1 + step // 2) % 2) * 2 + (y // 2 + 1 + step) % 2

    def add_shared(step):
        for h in range(2):
            chip = part_of(step) * 2 + h
            sib_copy(chip).wait_recv()
            total = (g_keep[chip] + g_sib[chip].astype(jnp.float32)).astype(jnp.bfloat16)
            g_sum[chip] = total

            @pl.when(chip % RING != y)
            def _():
                sum_copy(chip).start()

            @pl.when(chip % RING == y)
            def _():
                r_shared[chip] = total

    def product(which, at, matrix):
        dims = (((1,), (1,)), ((), ()))
        return lax.dot_general(y_wide[which, at, :], matrix[...], dims, preferred_element_type=jnp.float32)

    def send_terms(part, values):
        for n in range(4):
            target = part * 4 + n
            value = values[n * SLOT : n * SLOT + ROWS].astype(jnp.bfloat16)
            g_own[target] = value

            @pl.when(target % PLANE != here)
            def _():
                term_copy(target).start()

            @pl.when(target % PLANE == here)
            def _():
                r_own[target] = value

    shared_start = jnp.where(common >= 3, 0, 4)

    def terms(turn, _):
        step = turn % 4
        part = part_of(step)
        at = pl.ds(pl.multiple_of(part * PAD, PAD), PAD)
        shared_turn = turn // 4 == shared_start // 4

        @pl.when(paired & shared_turn)
        def _():
            values = product(0, at, ut_mat)
            for h in range(2):
                chip = part * 2 + h
                even = values[2 * h * SLOT : 2 * h * SLOT + ROWS]
                odd = values[(2 * h + 1) * SLOT : (2 * h + 1) * SLOT + ROWS]
                g_keep[chip] = jnp.where(k == 0, even, odd)
                g_give[chip] = jnp.where(k == 0, odd, even).astype(jnp.bfloat16)
                sib_copy(chip).start()

        @pl.when(paired & jnp.logical_not(shared_turn))
        def _():
            send_terms(part, product(1, at, u_mat))

        @pl.when(jnp.logical_not(paired) & (mine != NONE) & (turn < 4))
        def _():
            send_terms(part, product(0, at, u_mat) + product(0, at, ut_mat))

        @pl.when(paired & (turn > shared_start) & (turn <= shared_start + 4))
        def _():
            add_shared(turn - shared_start - 1)

        return 0

    lax.fori_loop(0, 8, terms, 0)

    @pl.when(paired & (shared_start == 4))
    def _():
        add_shared(3)

    def total_of(half, at, block):
        total = jnp.zeros((ROWS, WIDTH), jnp.float32)
        for source in range(PLANE):
            if OWN[half * PLANE + source] == block:
                @pl.when(here != source)
                def _():
                    remote(
                        g_own.at[0], r_own.at[at * PLANE + source], term_send.at[0],
                        term_recv.at[at * PLANE + source], {"col": sibling},
                    ).wait_recv()

                total = total + r_own[at * PLANE + source].astype(jnp.float32)
        for chip in range(RING):
            if SHARED[half * RING + chip] == block:
                @pl.when(y != chip)
                def _():
                    remote(
                        g_sum.at[0], r_shared.at[at * RING + chip], sum_send.at[0],
                        sum_recv.at[at * RING + chip], {"col": sibling},
                    ).wait_recv()

                total = total + r_shared[at * RING + chip].astype(jnp.float32)
        return total

    def back_copy(index, at):
        return remote(
            give_back.at[at, index], got_back.at[index], back_send.at[at * 3 + index], back_recv.at[index],
            {"row": ahead, "col": at * PLANE + here},
        )

    def cross_copy(index):
        return remote(
            give_across.at[index], got_across.at[index], cross_send.at[index], cross_recv.at[index],
            {"col": partner_z},
        )

    for half in range(2):
        @pl.when(z == half)
        def _():
            for at in (1 - half, half):
                for block in NEXT[half]:
                    give_back[at, block - 3] = total_of(half, at, block).astype(jnp.bfloat16)
                    back_copy(block - 3, at).start()
            for at in (1 - half, half):
                for index in range(3):
                    total = total_of(half, at, index)
                    if at == half:
                        out[index] = total
                    else:
                        give_across[index] = total.astype(jnp.bfloat16)
                        cross_copy(index).start()

    for index in range(3):
        cross_copy(index).wait_recv()
        back_copy(index, 0).wait_recv()
        out[index] += got_across[index].astype(jnp.float32) + got_back[index].astype(jnp.float32)

    ship_energy.wait_send()
    for index in range(3):
        cross(index).wait_send()
        ship(index, 0, 0).wait_send()
        cross_copy(index).wait_send()
    for half in range(2):
        @pl.when(z == half)
        def _():
            for at in range(2):
                for block in NEXT[half]:
                    back_copy(block - 3, at).wait_send()

    def drain(n, _):
        far, t = n // PLANE, n % PLANE
        target = z * PLANE + place(t)

        @pl.when((t > 0) & (own_of(target) != NONE))
        def _():
            own_copy(blocks, far, t, 0).wait_send()

        @pl.when((t > 0) & (t % 2 == 0) & (shared_of(target // 2) != NONE))
        def _():
            shared_copy(blocks, far, t, 0).wait_send()

        @pl.when((n % PLANE != here) & (mine != NONE))
        def _():
            term_copy(n).wait_send()

        return 0

    lax.fori_loop(0, COLS, drain, 0)

    @pl.when(paired)
    def _():
        def drain_chip(chip, _):
            hand(chip * 2 + k).wait_send()
            sib_copy(chip).wait_send()

            @pl.when(chip % RING != y)
            def _():
                sum_copy(chip).wait_send()

            return 0

        lax.fori_loop(0, CHIPS, drain_chip, 0)


def body(blocks, eps_occ, eps_vir, pairs):
    eps = eps_occ.reshape(1, 3 * ORB)
    vir = eps_vir.reshape(1, VIRT)
    slots = pairs.T
    anywhere = pl.BlockSpec(memory_space=pl.ANY)
    vmem = pl.BlockSpec(memory_space=pltpu.VMEM)
    bf16, f32 = jnp.bfloat16, jnp.float32
    dma = pltpu.SemaphoreType.DMA
    slab = (ROWS, WIDTH)
    return pl.pallas_call(
        kernel,
        out_shape=jax.ShapeDtypeStruct(blocks.shape, f32),
        in_specs=[anywhere] * 4,
        out_specs=vmem,
        scratch_shapes=[
            pltpu.VMEM((3,) + slab, bf16),
            pltpu.VMEM((2, 1, 3 * ORB), f32),
            pltpu.VMEM((1, VIRT), f32),
            pltpu.VMEM(slots.shape, jnp.int32),
            dma((4,)),
            pltpu.VMEM((3,) + slab, bf16),
            pltpu.VMEM((2, 3) + slab, bf16),
            pltpu.VMEM((2, ORB, PAD), f32),
            pltpu.VMEM((1, PAD), f32),
            pltpu.VMEM((COLS,) + slab, bf16),
            pltpu.VMEM((COLS,) + slab, bf16),
            pltpu.VMEM((2, FULL, WIDE), bf16),
            pltpu.VMEM((WIDTH, WIDE), bf16),
            pltpu.VMEM((WIDTH, WIDE), bf16),
            pltpu.VMEM((PAD, PAD), f32),
            pltpu.VMEM((8, 128), f32),
            pltpu.VMEM((COLS,) + slab, bf16),
            pltpu.VMEM((CHIPS,) + slab, f32),
            pltpu.VMEM((CHIPS,) + slab, bf16),
            pltpu.VMEM((CHIPS,) + slab, bf16),
            pltpu.VMEM((CHIPS,) + slab, bf16),
            pltpu.VMEM((COLS,) + slab, bf16),
            pltpu.VMEM((CHIPS,) + slab, bf16),
            pltpu.VMEM((2, 3) + slab, bf16),
            pltpu.VMEM((3,) + slab, bf16),
            pltpu.VMEM((3,) + slab, bf16),
            pltpu.VMEM((3,) + slab, bf16),
            dma((2,)), dma((3,)), dma((3,)), dma((3,)), dma((6,)),
            dma((COLS,)), dma((COLS,)), dma((CHIPS,)), dma((COLS,)), dma((CHIPS,)),
            dma((CHIPS,)), dma((CHIPS,)), dma((COLS,)), dma((COLS,)), dma((CHIPS,)), dma((CHIPS,)),
            dma((6,)), dma((3,)), dma((3,)), dma((3,)),
        ],
        compiler_params=pltpu.CompilerParams(
            collective_id=0, has_side_effects=True, vmem_limit_bytes=48 * 1024 * 1024
        ),
        cost_estimate=pl.CostEstimate(flops=6 * FULL**3, bytes_accessed=4 * 1024 * 1024, transcendentals=0),
    )(blocks, eps, vir, slots)


def solution(mesh):
    in_specs = (P("row", "col", None), P("row"), P(), P("row", None))
    out_specs = P("row", "col", None)
    return jax.shard_map(body, mesh=mesh, in_specs=in_specs, out_specs=out_specs, check_vma=False)
```
